128 devices in a mesh: row: 16 (over z_lo, y, core), col: 8 (over x, z_hi).
Axes of the slice: x: 4, y: 4, z: 4 (z_hi: 2, z_lo: 2; z = z_hi * 2 + z_lo), core: 2. Of those that a mesh axis runs over, the one named last changes fastest.
Arguments:
- amplitudes: float32 [16, 16, 1024, 1024], P(None, None, 'row', 'col'), may hold values from -6 to 6
- hole_ints: float32 [256, 256], replicated, may hold values from -0.375 to 0.375
- factors: bfloat16 [1024, 1024], replicated, may hold values from -0.1875 to 0.1875
- core_matrix: float32 [1024, 1024], replicated, may hold values from -5 to 5
Outputs:
- residual: float32 [16, 16, 1024, 1024], P(None, None, 'row', 'col')
The draws below stay inside these ranges and needn't reach their ends.
All inputs are finite; a program needn't handle non-finite values.
Results may differ from the reference program's by a relative error of at most 0.0046.
Values sent between devices are 32-bit elements; how exact they have to be, the bound alone decides.
No kernel may reach another device: no remote copies, remote signals or barrier semaphores. Data moves between devices by JAX's collectives and lax.ppermute only.
A program may use at most 128 MiB of HBM per device.

```python
import jax
import jax.numpy as jnp
from jax import lax

O = 16
V = 1024
NG = 1024
PAIRS = 256


def steps_of(rng, dims, shards, low, top_value):
    gain = 1.0
    for dim, parts in shards:
        draws = jax.random.uniform(jax.random.fold_in(jax.random.fold_in(rng, 6), dim), (parts,), jnp.float32, low / len(shards), top_value / len(shards))
        gain = gain * jnp.repeat(jnp.exp(draws), dims[dim] // parts).reshape((-1,) + (1,) * (len(dims) - 1 - dim))
    return gain


def centred(rng, shape, deviation, bound, split=(), held_as=jnp.bfloat16):
    factor_of = steps_of(rng, shape, split, -0.22, 0.18) if split else 1.0
    entries = jax.random.normal(rng, shape, jnp.float32) * deviation * factor_of
    return jnp.minimum(jnp.maximum(entries, -bound), bound).astype(held_as)


def setup_inputs(seed: int = 0) -> dict:
    key_of = jax.random.split(jax.random.key(seed), 5)
    return {
        "amplitudes": centred(key_of[0], (O, O, V, V), 1.0, 6.0, ((2, 16), (3, 8)), jnp.float32),
        "hole_ints": centred(key_of[1], (PAIRS, PAIRS), PAIRS ** -0.5, 0.375, (), jnp.float32),
        "factors": centred(key_of[2], (V, NG), V ** -0.5, 0.1875),
        "core_matrix": centred(key_of[3], (NG, NG), 1.0, 5.0, (), jnp.float32),
    }


def particle_ladder(matrix, factors, core_matrix):
    rounded = matrix.astype(jnp.bfloat16)
    left_side = jnp.dot(rounded, factors, preferred_element_type=jnp.float32).astype(jnp.bfloat16)
    inner = jnp.dot(factors.T, left_side, preferred_element_type=jnp.float32)
    weighted = (core_matrix * inner).astype(jnp.bfloat16)
    spread = jnp.dot(factors, weighted, preferred_element_type=jnp.float32).astype(jnp.bfloat16)
    return matrix + jnp.dot(spread, factors.T, preferred_element_type=jnp.float32)


def reference(amplitudes, hole_ints, factors, core_matrix):
    flattened = amplitudes.reshape(PAIRS, V * V)
    hole_term = jnp.dot(hole_ints, flattened, precision=lax.Precision.HIGHEST, preferred_element_type=jnp.float32)
    hole_term = hole_term.reshape(O, O, V, V)
    summed = hole_term + jnp.transpose(hole_term, (1, 0, 3, 2))
    summed = summed.reshape(PAIRS, V, V)
    result = lax.map(lambda matrix: particle_ladder(matrix, factors, core_matrix), summed)
    return result.reshape(O, O, V, V)
```

```python
import functools

import jax
import jax.numpy as jnp
import numpy as np
from jax import lax
from jax.experimental import pallas as pl
from jax.experimental.pallas import tpu as pltpu
from jax.sharding import PartitionSpec as P

AXES = ("row", "col")


def owned_pairs(occupied, devices):
    listing = []
    for i in range(occupied):
        for j in range(i + 1, occupied):
            listing += [i * occupied + j, j * occupied + i]
    for i in range(occupied):
        listing.append(i * occupied + i)
    assert len(listing) == 2 * devices
    return np.array(listing, dtype=np.int32)


def hole_kernel(weights_ref, order_ref, tiles_ref, out_ref, stacked):
    pairs = weights_ref.shape[0]

    @pl.when(pl.program_id(0) == 0)
    def _():
        weights = weights_ref[...]
        high = weights.astype(jnp.bfloat16)
        low = (weights - high.astype(jnp.float32)).astype(jnp.bfloat16)
        order = order_ref[...]
        high = jnp.dot(order, high, preferred_element_type=jnp.float32).astype(jnp.bfloat16)
        low = jnp.dot(order, low, preferred_element_type=jnp.float32).astype(jnp.bfloat16)
        stacked[:, 0:pairs] = high
        stacked[:, pairs : 2 * pairs] = high
        stacked[:, 2 * pairs : 3 * pairs] = low

    rows = tiles_ref.shape[1]
    width = tiles_ref.shape[2]
    source = tiles_ref.reshape(pairs * rows, width)
    target = out_ref.reshape(pairs * rows, width)
    for first in range(0, rows, 2):
        tile = jnp.concatenate(
            [source[pl.ds(first + k, pairs, stride=rows), :] for k in range(2)], axis=1
        )
        high = tile.astype(jnp.bfloat16)
        low = (tile - high.astype(jnp.float32)).astype(jnp.bfloat16)
        product = jnp.dot(
            stacked[...], jnp.concatenate([high, low, high], axis=0), preferred_element_type=jnp.float32
        )
        for k in range(2):
            target[pl.ds(first + k, pairs, stride=rows), :] = product[:, k * width : (k + 1) * width]


def hole_term(hole_ints, order, tiles):
    pairs, rows, width = tiles.shape
    step = 8
    return pl.pallas_call(
        hole_kernel,
        grid=(rows // step,),
        in_specs=[
            pl.BlockSpec((pairs, pairs), lambda i: (0, 0)),
            pl.BlockSpec((pairs, pairs), lambda i: (0, 0)),
            pl.BlockSpec((pairs, step, width), lambda i: (0, i, 0)),
        ],
        out_specs=pl.BlockSpec((pairs, step, width), lambda i: (0, i, 0)),
        out_shape=jax.ShapeDtypeStruct(tiles.shape, jnp.float32),
        scratch_shapes=[pltpu.VMEM((pairs, 3 * pairs), jnp.bfloat16)],
        compiler_params=pltpu.CompilerParams(vmem_limit_bytes=32 * 2**20),
        cost_estimate=pl.CostEstimate(
            flops=6 * pairs * pairs * rows * width, bytes_accessed=2 * tiles.size * 4, transcendentals=0
        ),
    )(hole_ints, order, tiles)


def ladder_kernel(first_diagonal, blocks_ref, factors_ref, turned_ref, core_ref, out_ref, summed, rounded, side, weighted):
    row_count, col_count, _, rows_local, cols_local = blocks_ref.shape
    virtual = row_count * rows_local
    device = lax.axis_index("row") * col_count + lax.axis_index("col")
    diagonal = (device >= first_diagonal).astype(jnp.int32)
    ratio = cols_local // rows_local
    chunk = 256
    for slot in range(2):
        partner = jnp.where(diagonal == 1, slot, 1 - slot)

        @pl.loop(0, col_count)
        def _(i):
            base = pl.multiple_of(i * cols_local, cols_local)
            for j in range(col_count):
                own = blocks_ref[pl.ds(i * ratio, ratio), j, slot].reshape(cols_local, cols_local)
                other = blocks_ref[j * ratio : (j + 1) * ratio, i, partner].reshape(cols_local, cols_local)
                total = own + other.T
                summed[slot, pl.ds(base, cols_local), j * cols_local : (j + 1) * cols_local] = total
                rounded[slot, pl.ds(base, cols_local), j * cols_local : (j + 1) * cols_local] = total.astype(jnp.bfloat16)

    for slot in range(2):

        @pl.loop(0, virtual // chunk)
        def _(i):
            here = pl.ds(pl.multiple_of(i * chunk, chunk), chunk)
            side[here, :] = jnp.dot(
                rounded[slot, here, :], factors_ref[...], preferred_element_type=jnp.float32
            ).astype(jnp.bfloat16)

        @pl.loop(0, virtual // chunk)
        def _(i):
            here = pl.ds(pl.multiple_of(i * chunk, chunk), chunk)
            inner = jnp.dot(turned_ref[here, :], side[...], preferred_element_type=jnp.float32)
            weighted[here, :] = (core_ref[here, :] * inner).astype(jnp.bfloat16)

        @pl.loop(0, virtual // chunk)
        def _(i):
            here = pl.ds(pl.multiple_of(i * chunk, chunk), chunk)
            side[here, :] = jnp.dot(
                factors_ref[here, :], weighted[...], preferred_element_type=jnp.float32
            ).astype(jnp.bfloat16)

        @pl.loop(0, virtual // chunk)
        def _(i):
            here = pl.ds(pl.multiple_of(i * chunk, chunk), chunk)
            result = summed[slot, here, :] + jnp.dot(side[here, :], turned_ref[...], preferred_element_type=jnp.float32)
            for r in range(chunk // rows_local):
                for c in range(col_count):
                    out_ref[i * (chunk // rows_local) + r, c, slot] = result[
                        r * rows_local : (r + 1) * rows_local, c * cols_local : (c + 1) * cols_local
                    ]


def ladder(blocks, factors, core_matrix, first_diagonal):
    virtual, grid_points = factors.shape
    full = pl.BlockSpec(memory_space=pltpu.VMEM)
    return pl.pallas_call(
        functools.partial(ladder_kernel, first_diagonal),
        in_specs=[full] * 4,
        out_specs=full,
        out_shape=jax.ShapeDtypeStruct(blocks.shape, jnp.float32),
        scratch_shapes=[
            pltpu.VMEM((2, virtual, virtual), jnp.float32),
            pltpu.VMEM((2, virtual, virtual), jnp.bfloat16),
            pltpu.VMEM((virtual, grid_points), jnp.bfloat16),
            pltpu.VMEM((grid_points, grid_points), jnp.bfloat16),
        ],
        compiler_params=pltpu.CompilerParams(vmem_limit_bytes=56 * 2**20),
        cost_estimate=pl.CostEstimate(
            flops=16 * virtual * virtual * grid_points, bytes_accessed=2 * blocks.size * 4, transcendentals=0
        ),
    )(blocks, factors, factors.T, core_matrix)


def place_kernel(places, in_ref, out_ref, sem):
    copies = [pltpu.make_async_copy(in_ref.at[p], out_ref.at[int(places[p])], sem.at[p]) for p in range(len(places))]
    for copy in copies:
        copy.start()
    for copy in copies:
        copy.wait()


def place(blocks, places):
    anywhere = pl.BlockSpec(memory_space=pl.ANY)
    return pl.pallas_call(
        functools.partial(place_kernel, places),
        in_specs=[anywhere],
        out_specs=anywhere,
        out_shape=jax.ShapeDtypeStruct(blocks.shape, blocks.dtype),
        scratch_shapes=[pltpu.SemaphoreType.DMA((len(places),))],
        compiler_params=pltpu.CompilerParams(vmem_limit_bytes=4 * 2**20),
        cost_estimate=pl.CostEstimate(flops=0, bytes_accessed=2 * blocks.size * 4, transcendentals=0),
    )(blocks)


def local(amplitudes, hole_ints, factors, core_matrix):
    row_count = lax.axis_size("row")
    col_count = lax.axis_size("col")
    devices = row_count * col_count
    occupied = amplitudes.shape[0]
    pairs = occupied * occupied
    rows_local, cols_local = amplitudes.shape[2:]
    owned = owned_pairs(occupied, devices)
    order = np.zeros((pairs, pairs), dtype=jnp.bfloat16)
    order[np.arange(pairs), owned] = 1
    hole = hole_term(hole_ints, jnp.asarray(order), amplitudes.reshape(pairs, rows_local, cols_local))
    moved = lax.all_to_all(
        hole.reshape(devices, 2, rows_local, cols_local), AXES, split_axis=0, concat_axis=0, tiled=True
    )
    result = ladder(
        moved.reshape(row_count, col_count, 2, rows_local, cols_local),
        factors,
        core_matrix,
        occupied * (occupied - 1) // 2,
    )
    returned = lax.all_to_all(
        result.reshape(devices, 2, rows_local, cols_local), AXES, split_axis=0, concat_axis=0, tiled=True
    )
    placed = place(returned.reshape(pairs, rows_local, cols_local), owned)
    return placed.reshape(occupied, occupied, rows_local, cols_local)


def solution(mesh):
    return jax.shard_map(
        local,
        mesh=mesh,
        in_specs=(P(None, None, "row", "col"), P(), P(), P()),
        out_specs=P(None, None, "row", "col"),
        check_vma=False,
    )
```

```python
import functools

import jax
import jax.numpy as jnp
import numpy as np
from jax import lax
from jax.experimental import pallas as pl
from jax.experimental.pallas import tpu as pltpu
from jax.sharding import PartitionSpec as P

AXES = ("row", "col")
MIB = 2**20


def owned_pairs(occupied, devices):
    listing = []
    for i in range(occupied):
        for j in range(i + 1, occupied):
            listing += [i * occupied + j, j * occupied + i]
    for i in range(occupied):
        listing.append(i * occupied + i)
    assert len(listing) == 2 * devices
    return np.array(listing, dtype=np.int32)


def in_vmem(array):
    return pltpu.with_memory_space_constraint(array, pltpu.VMEM)


def in_hbm(array):
    return pltpu.with_memory_space_constraint(array, pltpu.HBM)


WHOLE = pl.BlockSpec(memory_space=pltpu.VMEM)
ANYWHERE = pl.BlockSpec(memory_space=pl.ANY)


def hole_kernel(parts, weights_hbm, order_hbm, tiles_hbm, out_ref, weights_ref, order_ref, stacked, tiles, products, small_sem, in_sem, out_sem):
    pairs, rows, width = tiles_hbm.shape
    step = rows // parts
    pitch = tiles.shape[1]
    small = [
        pltpu.make_async_copy(weights_hbm, weights_ref, small_sem.at[0]),
        pltpu.make_async_copy(order_hbm, order_ref, small_sem.at[1]),
    ]
    incoming = [
        pltpu.make_async_copy(
            tiles_hbm.at[:, pl.ds(k * step, step), :], tiles.at[:, pl.ds(k * step, step), :], in_sem.at[k]
        )
        for k in range(parts)
    ]
    outgoing = [
        pltpu.make_async_copy(
            products.at[:, pl.ds(k * step, step), :], out_ref.at[:, pl.ds(k * step, step), :], out_sem.at[k]
        )
        for k in range(parts)
    ]
    for copy in small + incoming:
        copy.start()
    for copy in small:
        copy.wait()
    weights = weights_ref[...]
    high = weights.astype(jnp.bfloat16)
    low = (weights - high.astype(jnp.float32)).astype(jnp.bfloat16)
    order = order_ref[...]
    stacked[0:pairs, :] = jnp.dot(order, high, preferred_element_type=jnp.float32).astype(jnp.bfloat16)
    stacked[pairs : 2 * pairs, :] = jnp.dot(order, low, preferred_element_type=jnp.float32).astype(jnp.bfloat16)
    source = tiles.reshape(pairs * pitch, width)
    target = products.reshape(pairs * pitch, width)
    for k in range(parts):
        incoming[k].wait()
        for first in range(k * step, (k + 1) * step, 2):
            tile = jnp.concatenate(
                [source[pl.ds(first + q, pairs, stride=pitch), :] for q in range(2)], axis=1
            )
            high = tile.astype(jnp.bfloat16)
            low = (tile - high.astype(jnp.float32)).astype(jnp.bfloat16)
            both = jnp.dot(stacked[...], high, preferred_element_type=jnp.float32)
            rest = jnp.dot(stacked[0:pairs, :], low, preferred_element_type=jnp.float32)
            product = both[0:pairs] + (both[pairs : 2 * pairs] + rest)
            for q in range(2):
                target[pl.ds(first + q, pairs, stride=pitch), :] = product[:, q * width : (q + 1) * width]
        outgoing[k].start()
    for copy in outgoing:
        copy.wait()


def hole_term(hole_ints, order, tiles):
    pairs, rows, width = tiles.shape
    parts = 4
    pitched = (pairs, rows + 8, width)
    return pl.pallas_call(
        functools.partial(hole_kernel, parts),
        in_specs=[ANYWHERE] * 3,
        out_specs=WHOLE,
        out_shape=pltpu.VMEM(tiles.shape, jnp.float32),
        scratch_shapes=[
            pltpu.VMEM((pairs, pairs), jnp.float32),
            pltpu.VMEM((pairs, pairs), jnp.bfloat16),
            pltpu.VMEM((2 * pairs, pairs), jnp.bfloat16),
            pltpu.VMEM(pitched, jnp.float32),
            pltpu.VMEM(pitched, jnp.float32),
            pltpu.SemaphoreType.DMA((2,)),
            pltpu.SemaphoreType.DMA((parts,)),
            pltpu.SemaphoreType.DMA((parts,)),
        ],
        compiler_params=pltpu.CompilerParams(vmem_limit_bytes=22 * MIB),
        cost_estimate=pl.CostEstimate(
            flops=6 * pairs * pairs * rows * width, bytes_accessed=2 * tiles.size * 4, transcendentals=0
        ),
    )(in_hbm(hole_ints), in_hbm(order), in_hbm(tiles))


def ladder_kernel(first_diagonal, blocks_ref, factors_ref, core_ref, out_ref, rounded, turned, side, weighted):
    _, _, rows_local, cols_local = blocks_ref.shape
    virtual = factors_ref.shape[0]
    col_count = virtual // cols_local
    device = lax.axis_index("row") * col_count + lax.axis_index("col")
    diagonal = (device >= first_diagonal).astype(jnp.int32)
    ratio = cols_local // rows_local
    chunk = 256
    steps = virtual // chunk

    def rows_of(i, size=chunk):
        return slice(i * size, (i + 1) * size)

    def dot(a, b):
        return jnp.dot(a, b, preferred_element_type=jnp.float32)

    def square(i, j, slot):
        tiles = [blocks_ref[(i * ratio + r) * col_count + j, slot] for r in range(ratio)]
        return jnp.concatenate(tiles, axis=0)

    def build(slot, step):
        partner = jnp.where(diagonal == 1, slot, 1 - slot)
        for i in range(step * chunk // cols_local, (step + 1) * chunk // cols_local):
            for j in range(col_count):
                total = square(i, j, slot) + square(j, i, partner).T
                for r in range(ratio):
                    out_ref[(i * ratio + r) * col_count + j, slot] = total[rows_of(r, rows_local), :]
                rounded[slot, rows_of(i, cols_local), rows_of(j, cols_local)] = total.astype(jnp.bfloat16)

    def turn(step):
        turned[:, rows_of(step)] = factors_ref[rows_of(step), :].T

    def left(slot, step):
        side[slot, rows_of(step), :] = dot(rounded[slot, rows_of(step), :], factors_ref[...]).astype(jnp.bfloat16)

    def inner(slot, step):
        product = dot(turned[rows_of(step), :], side[slot])
        weighted[slot, rows_of(step), :] = (core_ref[rows_of(step), :] * product).astype(jnp.bfloat16)

    def spread(slot, step):
        side[slot, rows_of(step), :] = dot(factors_ref[rows_of(step), :], weighted[slot]).astype(jnp.bfloat16)

    def finish(slot, step):
        product = dot(side[slot, rows_of(step), :], turned[...])
        for r in range(chunk // rows_local):
            for c in range(col_count):
                place = (step * chunk // rows_local + r) * col_count + c
                out_ref[place, slot] = out_ref[place, slot] + product[rows_of(r, rows_local), rows_of(c, cols_local)]

    build(0, 0)
    for step in range(steps):
        if step + 1 < steps:
            build(0, step + 1)
        left(0, step)
        turn(step)
    for step in range(steps):
        build(1, step)
        inner(0, step)
    for step in range(steps):
        spread(0, step)
        left(1, step)
    for step in range(steps):
        finish(0, step)
        inner(1, step)
    for step in range(steps):
        spread(1, step)
    for step in range(steps):
        finish(1, step)


def ladder(blocks, factors, core_matrix, first_diagonal):
    virtual, grid_points = factors.shape
    return pl.pallas_call(
        functools.partial(ladder_kernel, first_diagonal),
        in_specs=[WHOLE] * 3,
        out_specs=WHOLE,
        out_shape=pltpu.VMEM(blocks.shape, jnp.float32),
        scratch_shapes=[
            pltpu.VMEM((2, virtual, virtual), jnp.bfloat16),
            pltpu.VMEM((grid_points, virtual), jnp.bfloat16),
            pltpu.VMEM((2, virtual, grid_points), jnp.bfloat16),
            pltpu.VMEM((2, grid_points, grid_points), jnp.bfloat16),
        ],
        compiler_params=pltpu.CompilerParams(vmem_limit_bytes=20 * MIB),
        cost_estimate=pl.CostEstimate(
            flops=16 * virtual * virtual * grid_points, bytes_accessed=2 * blocks.size * 4, transcendentals=0
        ),
    )(in_vmem(blocks), in_vmem(factors), in_vmem(core_matrix))


def place_moves(occupied):
    moves = []
    device = 0
    for i in range(occupied - 1):
        count = occupied - 1 - i
        moves.append((device, count, 0, i, i + 1, 1))
        moves.append((device, count, 1, i + 1, i, 0))
        device += count
    for i in range(occupied):
        moves.append((device + i // 2, 1, i % 2, i, i, 1))
    return moves


def place_kernel(moves, in_ref, out_ref, sem):
    copies = []
    for n, (device, count, slot, i, j, running) in enumerate(moves):
        source = in_ref.at[pl.ds(device, count), slot]
        target = out_ref.at[i, pl.ds(j, count)] if running == 1 else out_ref.at[pl.ds(i, count), j]
        copies.append(pltpu.make_async_copy(source, target, sem.at[n]))
    for copy in copies:
        copy.start()
    for copy in copies:
        copy.wait()


def place(blocks, occupied):
    moves = place_moves(occupied)
    return pl.pallas_call(
        functools.partial(place_kernel, moves),
        in_specs=[WHOLE],
        out_specs=ANYWHERE,
        out_shape=jax.ShapeDtypeStruct((occupied, occupied) + blocks.shape[2:], blocks.dtype),
        scratch_shapes=[pltpu.SemaphoreType.DMA((len(moves),))],
        compiler_params=pltpu.CompilerParams(vmem_limit_bytes=4 * MIB),
        cost_estimate=pl.CostEstimate(flops=0, bytes_accessed=2 * blocks.size * 4, transcendentals=0),
    )(in_vmem(blocks))


def exchange(blocks):
    return lax.all_to_all(blocks, AXES, split_axis=0, concat_axis=0, tiled=True)


def local(amplitudes, hole_ints, factors, core_matrix):
    row_count = lax.axis_size("row")
    col_count = lax.axis_size("col")
    devices = row_count * col_count
    occupied = amplitudes.shape[0]
    pairs = occupied * occupied
    rows_local, cols_local = amplitudes.shape[2:]
    order = np.zeros((pairs, pairs), dtype=jnp.bfloat16)
    order[np.arange(pairs), owned_pairs(occupied, devices)] = 1
    hole = hole_term(hole_ints, jnp.asarray(order), amplitudes.reshape(pairs, rows_local, cols_local))
    moved = exchange(hole.reshape(devices, 2, rows_local, cols_local))
    result = ladder(moved, factors, core_matrix, occupied * (occupied - 1) // 2)
    return place(exchange(result), occupied)


def solution(mesh):
    return jax.shard_map(
        local,
        mesh=mesh,
        in_specs=(P(None, None, "row", "col"), P(), P(), P()),
        out_specs=P(None, None, "row", "col"),
        check_vma=False,
    )
```

```python
import functools

import jax
import jax.numpy as jnp
import numpy as np
from jax import lax
from jax.experimental import pallas as pl
from jax.experimental.pallas import tpu as pltpu
from jax.sharding import PartitionSpec as P

AXES = ("row", "col")
MIB = 2**20


def owned_pairs(occupied, devices):
    listing = []
    for i in range(occupied):
        for j in range(i + 1, occupied):
            listing += [i * occupied + j, j * occupied + i]
    for i in range(occupied):
        listing.append(i * occupied + i)
    assert len(listing) == 2 * devices
    return np.array(listing, dtype=np.int32)


def in_vmem(array):
    return pltpu.with_memory_space_constraint(array, pltpu.VMEM)


def in_hbm(array):
    return pltpu.with_memory_space_constraint(array, pltpu.HBM)


WHOLE = pl.BlockSpec(memory_space=pltpu.VMEM)
ANYWHERE = pl.BlockSpec(memory_space=pl.ANY)


def hole_kernel(parts, weights_hbm, order_hbm, tiles_hbm, out_ref, weights_ref, order_ref, stacked, tiles, products, small_sem, in_sem, out_sem):
    pairs, rows, width = tiles_hbm.shape
    step = rows // parts
    pitch = tiles.shape[1]
    small = [
        pltpu.make_async_copy(weights_hbm, weights_ref, small_sem.at[0]),
        pltpu.make_async_copy(order_hbm, order_ref, small_sem.at[1]),
    ]
    incoming = [
        pltpu.make_async_copy(
            tiles_hbm.at[:, pl.ds(k * step, step), :], tiles.at[:, pl.ds(k * step, step), :], in_sem.at[k]
        )
        for k in range(parts)
    ]
    outgoing = [
        pltpu.make_async_copy(
            products.at[:, pl.ds(k * step, step), :], out_ref.at[:, pl.ds(k * step, step), :], out_sem.at[k]
        )
        for k in range(parts)
    ]
    ahead = 2
    for copy in small + incoming[:ahead]:
        copy.start()
    for copy in small:
        copy.wait()
    weights = weights_ref[...]
    high = weights.astype(jnp.bfloat16)
    low = (weights - high.astype(jnp.float32)).astype(jnp.bfloat16)
    order = order_ref[...]
    stacked[0:pairs, :] = jnp.dot(order, high, preferred_element_type=jnp.float32).astype(jnp.bfloat16)
    stacked[pairs : 2 * pairs, :] = jnp.dot(order, low, preferred_element_type=jnp.float32).astype(jnp.bfloat16)
    source = tiles.reshape(pairs * pitch, width)
    target = products.reshape(pairs * pitch, width)
    for k in range(parts):
        incoming[k].wait()
        if k + ahead < parts:
            incoming[k + ahead].start()
        for first in range(k * step, (k + 1) * step, 2):
            tile = jnp.concatenate(
                [source[pl.ds(first + q, pairs, stride=pitch), :] for q in range(2)], axis=1
            )
            high = tile.astype(jnp.bfloat16)
            low = (tile - high.astype(jnp.float32)).astype(jnp.bfloat16)
            both = jnp.dot(stacked[...], high, preferred_element_type=jnp.float32)
            rest = jnp.dot(stacked[0:pairs, :], low, preferred_element_type=jnp.float32)
            product = both[0:pairs] + (both[pairs : 2 * pairs] + rest)
            for q in range(2):
                target[pl.ds(first + q, pairs, stride=pitch), :] = product[:, q * width : (q + 1) * width]
        outgoing[k].start()
    for copy in outgoing:
        copy.wait()


def hole_term(hole_ints, order, tiles):
    pairs, rows, width = tiles.shape
    parts = 4
    pitched = (pairs, rows + 8, width)
    return pl.pallas_call(
        functools.partial(hole_kernel, parts),
        in_specs=[ANYWHERE] * 3,
        out_specs=WHOLE,
        out_shape=pltpu.VMEM(tiles.shape, jnp.float32),
        scratch_shapes=[
            pltpu.VMEM((pairs, pairs), jnp.float32),
            pltpu.VMEM((pairs, pairs), jnp.bfloat16),
            pltpu.VMEM((2 * pairs, pairs), jnp.bfloat16),
            pltpu.VMEM(pitched, jnp.float32),
            pltpu.VMEM(pitched, jnp.float32),
            pltpu.SemaphoreType.DMA((2,)),
            pltpu.SemaphoreType.DMA((parts,)),
            pltpu.SemaphoreType.DMA((parts,)),
        ],
        compiler_params=pltpu.CompilerParams(vmem_limit_bytes=22 * MIB),
        cost_estimate=pl.CostEstimate(
            flops=6 * pairs * pairs * rows * width, bytes_accessed=2 * tiles.size * 4, transcendentals=0
        ),
    )(in_hbm(hole_ints), in_hbm(order), in_hbm(tiles))


def ladder_kernel(first_diagonal, blocks_ref, factors_ref, core_ref, out_ref, rounded, turned, side, weighted, upper):
    _, _, rows_local, cols_local = blocks_ref.shape
    virtual, grid_points = factors_ref.shape
    col_count = virtual // cols_local
    device = lax.axis_index("row") * col_count + lax.axis_index("col")
    diagonal = (device >= first_diagonal).astype(jnp.int32)
    ratio = cols_local // rows_local
    chunk = 256
    steps = virtual // chunk

    def rows_of(i, size=chunk):
        return slice(i * size, (i + 1) * size)

    def dot(a, b):
        return jnp.dot(a, b, preferred_element_type=jnp.float32)

    def square(i, j, slot):
        tiles = [blocks_ref[(i * ratio + r) * col_count + j, slot] for r in range(ratio)]
        return jnp.concatenate(tiles, axis=0)

    def partner_of(slot):
        return jnp.where(diagonal == 1, slot, 1 - slot)

    def build(slot, step):
        partner = partner_of(slot)
        for i in range(step * chunk // cols_local, (step + 1) * chunk // cols_local):
            for j in range(col_count):
                total = square(i, j, slot) + square(j, i, partner).T
                for r in range(ratio):
                    out_ref[(i * ratio + r) * col_count + j, slot] = total[rows_of(r, rows_local), :]
                rounded[slot, rows_of(i, cols_local), rows_of(j, cols_local)] = total.astype(jnp.bfloat16)

    def turn(step):
        turned[:, rows_of(step)] = factors_ref[rows_of(step), :].T

    def left(slot, step):
        side[slot, rows_of(step), :] = dot(rounded[slot, rows_of(step), :], factors_ref[...]).astype(jnp.bfloat16)

    def block_number(i, j):
        return i * (2 * steps - i - 1) // 2 + j - i - 1

    def inner(slot, step):
        onward = slice(step * chunk, grid_points)
        product = dot(turned[rows_of(step), :], side[slot, :, onward])
        weighted[slot, rows_of(step), onward] = (core_ref[rows_of(step), onward] * product).astype(jnp.bfloat16)
        for j in range(step + 1, steps):
            upper[slot, block_number(step, j)] = product[:, rows_of(j - step)]

    def mirror(slot, step):
        for j in range(step + 1, steps):
            product = upper[partner_of(slot), block_number(step, j)].T
            weighted[slot, rows_of(j), rows_of(step)] = (core_ref[rows_of(j), rows_of(step)] * product).astype(jnp.bfloat16)

    def spread(slot, step):
        side[slot, rows_of(step), :] = dot(factors_ref[rows_of(step), :], weighted[slot]).astype(jnp.bfloat16)

    def finish(slot, step):
        product = dot(side[slot, rows_of(step), :], turned[...])
        for r in range(chunk // rows_local):
            for c in range(col_count):
                place = (step * chunk // rows_local + r) * col_count + c
                out_ref[place, slot] = out_ref[place, slot] + product[rows_of(r, rows_local), rows_of(c, cols_local)]

    build(0, 0)
    for step in range(steps):
        if step + 1 < steps:
            build(0, step + 1)
        left(0, step)
        turn(step)
    for step in range(steps):
        build(1, step)
        inner(0, step)
    for step in range(steps):
        left(1, step)
    for step in range(steps):
        inner(1, step)
        mirror(0, step)
    for step in range(steps):
        spread(0, step)
        mirror(1, step)
    for step in range(steps):
        finish(0, step)
        spread(1, step)
    for step in range(steps):
        finish(1, step)


def ladder(blocks, factors, core_matrix, first_diagonal):
    virtual, grid_points = factors.shape
    return pl.pallas_call(
        functools.partial(ladder_kernel, first_diagonal),
        in_specs=[WHOLE] * 3,
        out_specs=WHOLE,
        out_shape=pltpu.VMEM(blocks.shape, jnp.float32),
        scratch_shapes=[
            pltpu.VMEM((2, virtual, virtual), jnp.bfloat16),
            pltpu.VMEM((grid_points, virtual), jnp.bfloat16),
            pltpu.VMEM((2, virtual, grid_points), jnp.bfloat16),
            pltpu.VMEM((2, grid_points, grid_points), jnp.bfloat16),
            pltpu.VMEM((2, 6, 256, 256), jnp.float32),
        ],
        compiler_params=pltpu.CompilerParams(vmem_limit_bytes=22 * MIB),
        cost_estimate=pl.CostEstimate(
            flops=15 * virtual * virtual * grid_points, bytes_accessed=2 * blocks.size * 4, transcendentals=0
        ),
    )(in_vmem(blocks), in_vmem(factors), in_vmem(core_matrix))


def place_moves(occupied):
    moves = []
    device = 0
    for i in range(occupied - 1):
        count = occupied - 1 - i
        moves.append((device, count, 0, i, i + 1, 1))
        moves.append((device, count, 1, i + 1, i, 0))
        device += count
    for i in range(occupied):
        moves.append((device + i // 2, 1, i % 2, i, i, 1))
    return moves


def place_kernel(moves, in_ref, out_ref, sem):
    copies = []
    for n, (device, count, slot, i, j, running) in enumerate(moves):
        source = in_ref.at[pl.ds(device, count), slot]
        target = out_ref.at[i, pl.ds(j, count)] if running == 1 else out_ref.at[pl.ds(i, count), j]
        copies.append(pltpu.make_async_copy(source, target, sem.at[n]))
    for copy in copies:
        copy.start()
    for copy in copies:
        copy.wait()


def place(blocks, occupied):
    moves = place_moves(occupied)
    return pl.pallas_call(
        functools.partial(place_kernel, moves),
        in_specs=[WHOLE],
        out_specs=ANYWHERE,
        out_shape=jax.ShapeDtypeStruct((occupied, occupied) + blocks.shape[2:], blocks.dtype),
        scratch_shapes=[pltpu.SemaphoreType.DMA((len(moves),))],
        compiler_params=pltpu.CompilerParams(vmem_limit_bytes=4 * MIB),
        cost_estimate=pl.CostEstimate(flops=0, bytes_accessed=2 * blocks.size * 4, transcendentals=0),
    )(in_vmem(blocks))


def exchange(blocks):
    return lax.all_to_all(blocks, AXES, split_axis=0, concat_axis=0, tiled=True)


def local(amplitudes, hole_ints, factors, core_matrix):
    row_count = lax.axis_size("row")
    col_count = lax.axis_size("col")
    devices = row_count * col_count
    occupied = amplitudes.shape[0]
    pairs = occupied * occupied
    rows_local, cols_local = amplitudes.shape[2:]
    order = np.zeros((pairs, pairs), dtype=jnp.bfloat16)
    order[np.arange(pairs), owned_pairs(occupied, devices)] = 1
    hole = hole_term(hole_ints, jnp.asarray(order), amplitudes.reshape(pairs, rows_local, cols_local))
    moved = exchange(hole.reshape(devices, 2, rows_local, cols_local))
    result = ladder(moved, factors, core_matrix, occupied * (occupied - 1) // 2)
    return place(exchange(result), occupied)


def solution(mesh):
    return jax.shard_map(
        local,
        mesh=mesh,
        in_specs=(P(None, None, "row", "col"), P(), P(), P()),
        out_specs=P(None, None, "row", "col"),
        check_vma=False,
    )
```

```python
import functools

import jax
import jax.numpy as jnp
import numpy as np
from jax import lax
from jax.experimental import pallas as pl
from jax.experimental.pallas import tpu as pltpu
from jax.sharding import PartitionSpec as P

AXES = ("row", "col")
MIB = 2**20


def owned_pairs(occupied, devices):
    listing = []
    for i in range(occupied):
        for j in range(i + 1, occupied):
            listing += [i * occupied + j, j * occupied + i]
    for i in range(occupied):
        listing.append(i * occupied + i)
    assert len(listing) == 2 * devices
    return np.array(listing, dtype=np.int32)


def in_vmem(array):
    return pltpu.with_memory_space_constraint(array, pltpu.VMEM)


def in_hbm(array):
    return pltpu.with_memory_space_constraint(array, pltpu.HBM)


WHOLE = pl.BlockSpec(memory_space=pltpu.VMEM)
ANYWHERE = pl.BlockSpec(memory_space=pl.ANY)


def hole_kernel(parts, weights_hbm, order_hbm, tiles_hbm, out_ref, weights_ref, order_ref, stacked, tiles, products, small_sem, in_sem, out_sem):
    pairs, rows, width = tiles_hbm.shape
    held, pitch, _ = tiles.shape
    spans = [(sum(parts[:k]), parts[k]) for k in range(len(parts))]
    small = [
        pltpu.make_async_copy(weights_hbm, weights_ref, small_sem.at[0]),
        pltpu.make_async_copy(order_hbm, order_ref, small_sem.at[1]),
    ]
    incoming = [
        pltpu.make_async_copy(
            tiles_hbm.at[:, pl.ds(first, count), :], tiles.at[pl.ds(0, pairs), pl.ds(first, count), :], in_sem.at[k]
        )
        for k, (first, count) in enumerate(spans)
    ]
    outgoing = [
        pltpu.make_async_copy(
            products.at[pl.ds(0, pairs), pl.ds(first, count), :], out_ref.at[:, pl.ds(first, count), :], out_sem.at[k]
        )
        for k, (first, count) in enumerate(spans)
    ]
    ahead = 2
    for copy in small + incoming[:ahead]:
        copy.start()
    for copy in small:
        copy.wait()
    weights = weights_ref[...]
    high = weights.astype(jnp.bfloat16)
    low = (weights - high.astype(jnp.float32)).astype(jnp.bfloat16)
    order = order_ref[...]
    stacked[0:pairs, :] = jnp.dot(order, high, preferred_element_type=jnp.float32).astype(jnp.bfloat16)
    stacked[pairs : 2 * pairs, :] = jnp.dot(order, low, preferred_element_type=jnp.float32).astype(jnp.bfloat16)
    source = tiles.reshape(held * pitch, width)
    target = products.reshape(held * pitch, width)
    for k, (first, count) in enumerate(spans):
        incoming[k].wait()
        if k + ahead < len(parts):
            incoming[k + ahead].start()
        for row in range(first, first + count, 2):
            tile = jnp.concatenate(
                [source[pl.ds(row + q, pairs, stride=pitch), :] for q in range(2)], axis=1
            )
            high = tile.astype(jnp.bfloat16)
            low = (tile - high.astype(jnp.float32)).astype(jnp.bfloat16)
            both = jnp.dot(stacked[...], high, preferred_element_type=jnp.float32)
            rest = jnp.dot(stacked[0:pairs, :], low, preferred_element_type=jnp.float32)
            product = both[0:pairs] + (both[pairs : 2 * pairs] + rest)
            for q in range(2):
                target[pl.ds(row + q, pairs, stride=pitch), :] = product[:, q * width : (q + 1) * width]
        outgoing[k].start()
    for copy in outgoing:
        copy.wait()


def hole_term(hole_ints, order, tiles):
    pairs, rows, width = tiles.shape
    parts = (rows // 8, 3 * rows // 8, rows // 2)
    pitched = (pairs + 1, rows + 8, width)
    return pl.pallas_call(
        functools.partial(hole_kernel, parts),
        in_specs=[ANYWHERE] * 3,
        out_specs=WHOLE,
        out_shape=pltpu.VMEM(tiles.shape, jnp.float32),
        scratch_shapes=[
            pltpu.VMEM((pairs, pairs), jnp.float32),
            pltpu.VMEM((pairs, pairs), jnp.bfloat16),
            pltpu.VMEM((2 * pairs, pairs), jnp.bfloat16),
            pltpu.VMEM(pitched, jnp.float32),
            pltpu.VMEM(pitched, jnp.float32),
            pltpu.SemaphoreType.DMA((2,)),
            pltpu.SemaphoreType.DMA((len(parts),)),
            pltpu.SemaphoreType.DMA((len(parts),)),
        ],
        compiler_params=pltpu.CompilerParams(vmem_limit_bytes=22 * MIB),
        cost_estimate=pl.CostEstimate(
            flops=6 * pairs * pairs * rows * width, bytes_accessed=2 * tiles.size * 4, transcendentals=0
        ),
    )(in_hbm(hole_ints), in_hbm(order), in_hbm(tiles))


def ladder_kernel(first_diagonal, blocks_ref, factors_ref, core_ref, out_ref, rounded, turned, side, weighted, upper):
    _, _, rows_local, cols_local = blocks_ref.shape
    virtual, grid_points = factors_ref.shape
    col_count = virtual // cols_local
    device = lax.axis_index("row") * col_count + lax.axis_index("col")
    diagonal = (device >= first_diagonal).astype(jnp.int32)
    ratio = cols_local // rows_local
    chunk = 256
    steps = virtual // chunk

    def rows_of(i, size=chunk):
        return slice(i * size, (i + 1) * size)

    def dot(a, b):
        return jnp.dot(a, b, preferred_element_type=jnp.float32)

    def square(i, j, slot):
        tiles = [blocks_ref[(i * ratio + r) * col_count + j, slot] for r in range(ratio)]
        return jnp.concatenate(tiles, axis=0)

    def partner_of(slot):
        return jnp.where(diagonal == 1, slot, 1 - slot)

    def build(slot, step):
        partner = partner_of(slot)
        for i in range(step * chunk // cols_local, (step + 1) * chunk // cols_local):
            for j in range(col_count):
                total = square(i, j, slot) + square(j, i, partner).T
                for r in range(ratio):
                    out_ref[(i * ratio + r) * col_count + j, slot] = total[rows_of(r, rows_local), :]
                rounded[slot, rows_of(i, cols_local), rows_of(j, cols_local)] = total.astype(jnp.bfloat16)

    def turn(step):
        turned[:, rows_of(step)] = factors_ref[rows_of(step), :].T

    def left(slot, step):
        side[slot, rows_of(step), :] = dot(rounded[slot, rows_of(step), :], factors_ref[...]).astype(jnp.bfloat16)

    def block_number(i, j):
        return i * (2 * steps - i - 1) // 2 + j - i - 1

    def inner(slot, step):
        onward = slice(step * chunk, grid_points)
        product = dot(turned[rows_of(step), :], side[slot, :, onward])
        weighted[slot, rows_of(step), onward] = (core_ref[rows_of(step), onward] * product).astype(jnp.bfloat16)
        for j in range(step + 1, steps):
            upper[slot, block_number(step, j)] = product[:, rows_of(j - step)]

    def mirror(slot, step):
        for j in range(step + 1, steps):
            product = upper[partner_of(slot), block_number(step, j)].T
            weighted[slot, rows_of(j), rows_of(step)] = (core_ref[rows_of(j), rows_of(step)] * product).astype(jnp.bfloat16)

    def spread(slot, step):
        side[slot, rows_of(step), :] = dot(factors_ref[rows_of(step), :], weighted[slot]).astype(jnp.bfloat16)

    def finish(slot, step):
        product = dot(side[slot, rows_of(step), :], turned[...])
        for r in range(chunk // rows_local):
            for c in range(col_count):
                place = (step * chunk // rows_local + r) * col_count + c
                out_ref[place, slot] = out_ref[place, slot] + product[rows_of(r, rows_local), rows_of(c, cols_local)]

    build(0, 0)
    for step in range(steps):
        if step + 1 < steps:
            build(0, step + 1)
        left(0, step)
        turn(step)
    for step in range(steps):
        build(1, step)
        inner(0, step)
    for step in range(steps):
        left(1, step)
    for step in range(steps):
        inner(1, step)
        mirror(0, step)
    for step in range(steps):
        spread(0, step)
        mirror(1, step)
    for step in range(steps):
        finish(0, step)
        spread(1, step)
    for step in range(steps):
        finish(1, step)


def ladder(blocks, factors, core_matrix, first_diagonal):
    virtual, grid_points = factors.shape
    return pl.pallas_call(
        functools.partial(ladder_kernel, first_diagonal),
        in_specs=[WHOLE] * 3,
        out_specs=WHOLE,
        out_shape=pltpu.VMEM(blocks.shape, jnp.float32),
        scratch_shapes=[
            pltpu.VMEM((2, virtual, virtual), jnp.bfloat16),
            pltpu.VMEM((grid_points, virtual), jnp.bfloat16),
            pltpu.VMEM((2, virtual, grid_points), jnp.bfloat16),
            pltpu.VMEM((2, grid_points, grid_points), jnp.bfloat16),
            pltpu.VMEM((2, 6, 256, 256), jnp.float32),
        ],
        compiler_params=pltpu.CompilerParams(vmem_limit_bytes=22 * MIB),
        cost_estimate=pl.CostEstimate(
            flops=15 * virtual * virtual * grid_points, bytes_accessed=2 * blocks.size * 4, transcendentals=0
        ),
    )(in_vmem(blocks), in_vmem(factors), in_vmem(core_matrix))


def place_moves(occupied):
    moves = []
    device = 0
    for i in range(occupied - 1):
        count = occupied - 1 - i
        moves.append((device, count, 0, i, i + 1, 1))
        moves.append((device, count, 1, i + 1, i, 0))
        device += count
    for i in range(occupied):
        moves.append((device + i // 2, 1, i % 2, i, i, 1))
    return moves


def place_kernel(moves, in_ref, out_ref, sem):
    copies = []
    for n, (device, count, slot, i, j, running) in enumerate(moves):
        source = in_ref.at[pl.ds(device, count), slot]
        target = out_ref.at[i, pl.ds(j, count)] if running == 1 else out_ref.at[pl.ds(i, count), j]
        copies.append(pltpu.make_async_copy(source, target, sem.at[n]))
    for copy in copies:
        copy.start()
    for copy in copies:
        copy.wait()


def place(blocks, occupied):
    moves = place_moves(occupied)
    return pl.pallas_call(
        functools.partial(place_kernel, moves),
        in_specs=[WHOLE],
        out_specs=ANYWHERE,
        out_shape=jax.ShapeDtypeStruct((occupied, occupied) + blocks.shape[2:], blocks.dtype),
        scratch_shapes=[pltpu.SemaphoreType.DMA((len(moves),))],
        compiler_params=pltpu.CompilerParams(vmem_limit_bytes=4 * MIB),
        cost_estimate=pl.CostEstimate(flops=0, bytes_accessed=2 * blocks.size * 4, transcendentals=0),
    )(in_vmem(blocks))


def exchange(blocks):
    return lax.all_to_all(blocks, AXES, split_axis=0, concat_axis=0, tiled=True)


def local(amplitudes, hole_ints, factors, core_matrix):
    row_count = lax.axis_size("row")
    col_count = lax.axis_size("col")
    devices = row_count * col_count
    occupied = amplitudes.shape[0]
    pairs = occupied * occupied
    rows_local, cols_local = amplitudes.shape[2:]
    order = np.zeros((pairs, pairs), dtype=jnp.bfloat16)
    order[np.arange(pairs), owned_pairs(occupied, devices)] = 1
    hole = hole_term(hole_ints, jnp.asarray(order), amplitudes.reshape(pairs, rows_local, cols_local))
    moved = exchange(hole.reshape(devices, 2, rows_local, cols_local))
    result = ladder(moved, factors, core_matrix, occupied * (occupied - 1) // 2)
    return place(exchange(result), occupied)


def solution(mesh):
    return jax.shard_map(
        local,
        mesh=mesh,
        in_specs=(P(None, None, "row", "col"), P(), P(), P()),
        out_specs=P(None, None, "row", "col"),
        check_vma=False,
    )
```

```python
import functools

import jax
import jax.numpy as jnp
import numpy as np
from jax import lax
from jax.experimental import pallas as pl
from jax.experimental.pallas import tpu as pltpu
from jax.sharding import PartitionSpec as P

AXES = ("row", "col")
MIB = 2**20


def owned_pairs(occupied, devices):
    listing = []
    for i in range(occupied):
        for j in range(i + 1, occupied):
            listing += [i * occupied + j, j * occupied + i]
    for i in range(occupied):
        listing.append(i * occupied + i)
    assert len(listing) == 2 * devices
    return np.array(listing, dtype=np.int32)


def in_vmem(array):
    return pltpu.with_memory_space_constraint(array, pltpu.VMEM)


def in_hbm(array):
    return pltpu.with_memory_space_constraint(array, pltpu.HBM)


WHOLE = pl.BlockSpec(memory_space=pltpu.VMEM)
ANYWHERE = pl.BlockSpec(memory_space=pl.ANY)


def hole_kernel(parts, weights_hbm, order_hbm, tiles_hbm, out_ref, weights_ref, order_ref, stacked, tiles, products, small_sem, in_sem, out_sem):
    pairs, rows, width = tiles_hbm.shape
    held, pitch, _ = tiles.shape
    spans = [(sum(parts[:k]), parts[k]) for k in range(len(parts))]
    small = [
        pltpu.make_async_copy(weights_hbm, weights_ref, small_sem.at[0]),
        pltpu.make_async_copy(order_hbm, order_ref, small_sem.at[1]),
    ]
    incoming = [
        pltpu.make_async_copy(
            tiles_hbm.at[:, pl.ds(first, count), :], tiles.at[pl.ds(0, pairs), pl.ds(first, count), :], in_sem.at[k]
        )
        for k, (first, count) in enumerate(spans)
    ]
    outgoing = [
        pltpu.make_async_copy(
            products.at[pl.ds(0, pairs), pl.ds(first, count), :], out_ref.at[:, pl.ds(first, count), :], out_sem.at[k]
        )
        for k, (first, count) in enumerate(spans)
    ]
    for copy in small + incoming[:1]:
        copy.start()
    for copy in incoming[1:]:
        copy.start(priority=1)
    for copy in small:
        copy.wait()
    weights = weights_ref[...]
    high = weights.astype(jnp.bfloat16)
    low = (weights - high.astype(jnp.float32)).astype(jnp.bfloat16)
    order = order_ref[...]
    stacked[0:pairs, :] = jnp.dot(order, high, preferred_element_type=jnp.float32).astype(jnp.bfloat16)
    stacked[pairs : 2 * pairs, :] = jnp.dot(order, low, preferred_element_type=jnp.float32).astype(jnp.bfloat16)
    source = tiles.reshape(held * pitch, width)
    target = products.reshape(held * pitch, width)
    for k, (first, count) in enumerate(spans):
        incoming[k].wait()
        for row in range(first, first + count, 2):
            tile = jnp.concatenate(
                [source[pl.ds(row + q, pairs, stride=pitch), :] for q in range(2)], axis=1
            )
            high = tile.astype(jnp.bfloat16)
            low = (tile - high.astype(jnp.float32)).astype(jnp.bfloat16)
            both = jnp.dot(stacked[...], high, preferred_element_type=jnp.float32)
            rest = jnp.dot(stacked[0:pairs, :], low, preferred_element_type=jnp.float32)
            product = both[0:pairs] + (both[pairs : 2 * pairs] + rest)
            for q in range(2):
                target[pl.ds(row + q, pairs, stride=pitch), :] = product[:, q * width : (q + 1) * width]
        outgoing[k].start()
    for copy in outgoing:
        copy.wait()


def hole_term(hole_ints, order, tiles):
    pairs, rows, width = tiles.shape
    parts = (rows // 8, 3 * rows // 8, rows // 2)
    pitched = (pairs + 1, rows + 8, width)
    return pl.pallas_call(
        functools.partial(hole_kernel, parts),
        in_specs=[ANYWHERE] * 3,
        out_specs=WHOLE,
        out_shape=pltpu.VMEM(tiles.shape, jnp.float32),
        scratch_shapes=[
            pltpu.VMEM((pairs, pairs), jnp.float32),
            pltpu.VMEM((pairs, pairs), jnp.bfloat16),
            pltpu.VMEM((2 * pairs, pairs), jnp.bfloat16),
            pltpu.VMEM(pitched, jnp.float32),
            pltpu.VMEM(pitched, jnp.float32),
            pltpu.SemaphoreType.DMA((2,)),
            pltpu.SemaphoreType.DMA((len(parts),)),
            pltpu.SemaphoreType.DMA((len(parts),)),
        ],
        compiler_params=pltpu.CompilerParams(vmem_limit_bytes=22 * MIB),
        cost_estimate=pl.CostEstimate(
            flops=6 * pairs * pairs * rows * width, bytes_accessed=2 * tiles.size * 4, transcendentals=0
        ),
    )(in_hbm(hole_ints), in_hbm(order), in_hbm(tiles))


def ladder_kernel(first_diagonal, blocks_ref, factors_ref, core_ref, out_ref, rounded, turned, side, weighted, upper):
    _, _, rows_local, cols_local = blocks_ref.shape
    virtual, grid_points = factors_ref.shape
    col_count = virtual // cols_local
    device = lax.axis_index("row") * col_count + lax.axis_index("col")
    diagonal = (device >= first_diagonal).astype(jnp.int32)
    ratio = cols_local // rows_local
    chunk = 256
    steps = virtual // chunk

    def rows_of(i, size=chunk):
        return slice(i * size, (i + 1) * size)

    def dot(a, b):
        return jnp.dot(a, b, preferred_element_type=jnp.float32)

    def square(i, j, slot):
        tiles = [blocks_ref[(i * ratio + r) * col_count + j, slot] for r in range(ratio)]
        return jnp.concatenate(tiles, axis=0)

    def partner_of(slot):
        return jnp.where(diagonal == 1, slot, 1 - slot)

    def build(slot, step):
        partner = partner_of(slot)
        for i in range(step * chunk // cols_local, (step + 1) * chunk // cols_local):
            for j in range(col_count):
                total = square(i, j, slot) + square(j, i, partner).T
                for r in range(ratio):
                    out_ref[(i * ratio + r) * col_count + j, slot] = total[rows_of(r, rows_local), :]
                rounded[slot, rows_of(i, cols_local), rows_of(j, cols_local)] = total.astype(jnp.bfloat16)

    def turn(step):
        turned[:, rows_of(step)] = factors_ref[rows_of(step), :].T

    def left(slot, step):
        side[slot, rows_of(step), :] = dot(rounded[slot, rows_of(step), :], factors_ref[...]).astype(jnp.bfloat16)

    def block_number(i, j):
        return i * (2 * steps - i - 1) // 2 + j - i - 1

    def inner(slot, step):
        onward = slice(step * chunk, grid_points)
        product = dot(turned[rows_of(step), :], side[slot, :, onward])
        weighted[slot, rows_of(step), onward] = (core_ref[rows_of(step), onward] * product).astype(jnp.bfloat16)
        for j in range(step + 1, steps):
            upper[slot, block_number(step, j)] = product[:, rows_of(j - step)]

    def mirror(slot, step):
        for j in range(step + 1, steps):
            product = upper[partner_of(slot), block_number(step, j)].T
            weighted[slot, rows_of(j), rows_of(step)] = (core_ref[rows_of(j), rows_of(step)] * product).astype(jnp.bfloat16)

    def spread(slot, step):
        side[slot, rows_of(step), :] = dot(factors_ref[rows_of(step), :], weighted[slot]).astype(jnp.bfloat16)

    def finish(slot, step):
        product = dot(side[slot, rows_of(step), :], turned[...])
        for r in range(chunk // rows_local):
            for c in range(col_count):
                place = (step * chunk // rows_local + r) * col_count + c
                out_ref[place, slot] = out_ref[place, slot] + product[rows_of(r, rows_local), rows_of(c, cols_local)]

    build(0, 0)
    for step in range(steps):
        if step + 1 < steps:
            build(0, step + 1)
        left(0, step)
        turn(step)
    for step in range(steps):
        build(1, step)
        inner(0, step)
    for step in range(steps):
        left(1, step)
    for step in range(steps):
        inner(1, step)
        mirror(0, step)
    for step in range(steps):
        spread(0, step)
        mirror(1, step)
    for step in range(steps):
        finish(0, step)
        spread(1, step)
    for step in range(steps):
        finish(1, step)


def ladder(blocks, factors, core_matrix, first_diagonal):
    virtual, grid_points = factors.shape
    return pl.pallas_call(
        functools.partial(ladder_kernel, first_diagonal),
        in_specs=[WHOLE] * 3,
        out_specs=WHOLE,
        out_shape=pltpu.VMEM(blocks.shape, jnp.float32),
        scratch_shapes=[
            pltpu.VMEM((2, virtual, virtual), jnp.bfloat16),
            pltpu.VMEM((grid_points, virtual), jnp.bfloat16),
            pltpu.VMEM((2, virtual, grid_points), jnp.bfloat16),
            pltpu.VMEM((2, grid_points, grid_points), jnp.bfloat16),
            pltpu.VMEM((2, 6, 256, 256), jnp.float32),
        ],
        compiler_params=pltpu.CompilerParams(vmem_limit_bytes=22 * MIB),
        cost_estimate=pl.CostEstimate(
            flops=15 * virtual * virtual * grid_points, bytes_accessed=2 * blocks.size * 4, transcendentals=0
        ),
    )(in_vmem(blocks), in_vmem(factors), in_vmem(core_matrix))


def place_moves(occupied):
    moves = []
    device = 0
    for i in range(occupied - 1):
        count = occupied - 1 - i
        moves.append((device, count, 0, i, i + 1, 1))
        moves.append((device, count, 1, i + 1, i, 0))
        device += count
    for i in range(occupied):
        moves.append((device + i // 2, 1, i % 2, i, i, 1))
    return moves


def place_kernel(moves, in_ref, out_ref, sem):
    copies = []
    for n, (device, count, slot, i, j, running) in enumerate(moves):
        source = in_ref.at[pl.ds(device, count), slot]
        target = out_ref.at[i, pl.ds(j, count)] if running == 1 else out_ref.at[pl.ds(i, count), j]
        copies.append(pltpu.make_async_copy(source, target, sem.at[n]))
    for copy in copies:
        copy.start()
    for copy in copies:
        copy.wait()


def place(blocks, occupied):
    moves = place_moves(occupied)
    return pl.pallas_call(
        functools.partial(place_kernel, moves),
        in_specs=[WHOLE],
        out_specs=ANYWHERE,
        out_shape=jax.ShapeDtypeStruct((occupied, occupied) + blocks.shape[2:], blocks.dtype),
        scratch_shapes=[pltpu.SemaphoreType.DMA((len(moves),))],
        compiler_params=pltpu.CompilerParams(vmem_limit_bytes=4 * MIB),
        cost_estimate=pl.CostEstimate(flops=0, bytes_accessed=2 * blocks.size * 4, transcendentals=0),
    )(in_vmem(blocks))


def exchange(blocks):
    return lax.all_to_all(blocks, AXES, split_axis=0, concat_axis=0, tiled=True)


def local(amplitudes, hole_ints, factors, core_matrix):
    row_count = lax.axis_size("row")
    col_count = lax.axis_size("col")
    devices = row_count * col_count
    occupied = amplitudes.shape[0]
    pairs = occupied * occupied
    rows_local, cols_local = amplitudes.shape[2:]
    order = np.zeros((pairs, pairs), dtype=jnp.bfloat16)
    order[np.arange(pairs), owned_pairs(occupied, devices)] = 1
    hole = hole_term(hole_ints, jnp.asarray(order), amplitudes.reshape(pairs, rows_local, cols_local))
    moved = exchange(hole.reshape(devices, 2, rows_local, cols_local))
    result = ladder(moved, factors, core_matrix, occupied * (occupied - 1) // 2)
    return place(exchange(result), occupied)


def solution(mesh):
    return jax.shard_map(
        local,
        mesh=mesh,
        in_specs=(P(None, None, "row", "col"), P(), P(), P()),
        out_specs=P(None, None, "row", "col"),
        check_vma=False,
    )
```

```python
import functools

import jax
import jax.numpy as jnp
import numpy as np
from jax import lax
from jax.experimental import pallas as pl
from jax.experimental.pallas import tpu as pltpu
from jax.sharding import PartitionSpec as P

AXES = ("row", "col")
MIB = 2**20


def owned_pairs(occupied, devices):
    listing = []
    for i in range(occupied):
        for j in range(i + 1, occupied):
            listing += [i * occupied + j, j * occupied + i]
    for i in range(occupied):
        listing.append(i * occupied + i)
    assert len(listing) == 2 * devices
    return np.array(listing, dtype=np.int32)


def in_vmem(array):
    return pltpu.with_memory_space_constraint(array, pltpu.VMEM)


def in_hbm(array):
    return pltpu.with_memory_space_constraint(array, pltpu.HBM)


WHOLE = pl.BlockSpec(memory_space=pltpu.VMEM)
ANYWHERE = pl.BlockSpec(memory_space=pl.ANY)


def hole_kernel(parts, weights_hbm, order_hbm, tiles_hbm, out_ref, weights_ref, order_ref, stacked, tiles, products, small_sem, in_sem, out_sem):
    pairs, rows, width = tiles_hbm.shape
    held, pitch, _ = tiles.shape
    spans = [(sum(parts[:k]), parts[k]) for k in range(len(parts))]
    small = [
        pltpu.make_async_copy(weights_hbm, weights_ref, small_sem.at[0]),
        pltpu.make_async_copy(order_hbm, order_ref, small_sem.at[1]),
    ]
    incoming = [
        pltpu.make_async_copy(
            tiles_hbm.at[:, pl.ds(first, count), :], tiles.at[pl.ds(0, pairs), pl.ds(first, count), :], in_sem.at[k]
        )
        for k, (first, count) in enumerate(spans)
    ]
    outgoing = [
        pltpu.make_async_copy(
            products.at[pl.ds(0, pairs), pl.ds(first, count), :], out_ref.at[:, pl.ds(first, count), :], out_sem.at[k]
        )
        for k, (first, count) in enumerate(spans)
    ]
    ahead = 2
    for copy in small + incoming[:ahead]:
        copy.start()
    for copy in small:
        copy.wait()
    weights = weights_ref[...]
    high = weights.astype(jnp.bfloat16)
    low = (weights - high.astype(jnp.float32)).astype(jnp.bfloat16)
    order = order_ref[...]
    stacked[0:pairs, :] = jnp.dot(order, high, preferred_element_type=jnp.float32).astype(jnp.bfloat16)
    stacked[pairs : 2 * pairs, :] = jnp.dot(order, low, preferred_element_type=jnp.float32).astype(jnp.bfloat16)
    source = tiles.reshape(held * pitch, width)
    target = products.reshape(held * pitch, width)
    for k, (first, count) in enumerate(spans):
        incoming[k].wait()
        if k + ahead < len(parts):
            incoming[k + ahead].start()
        for row in range(first, first + count, 2):
            tile = jnp.concatenate(
                [source[pl.ds(row + q, pairs, stride=pitch), :] for q in range(2)], axis=1
            )
            high = tile.astype(jnp.bfloat16)
            low = (tile - high.astype(jnp.float32)).astype(jnp.bfloat16)
            both = jnp.dot(stacked[...], high, preferred_element_type=jnp.float32)
            rest = jnp.dot(stacked[0:pairs, :], low, preferred_element_type=jnp.float32)
            product = both[0:pairs] + (both[pairs : 2 * pairs] + rest)
            for q in range(2):
                target[pl.ds(row + q, pairs, stride=pitch), :] = product[:, q * width : (q + 1) * width]
        outgoing[k].start()
    for copy in outgoing:
        copy.wait()


def hole_term(hole_ints, order, tiles):
    pairs, rows, width = tiles.shape
    parts = (rows // 8, 3 * rows // 8, rows // 2)
    pitched = (pairs + 1, rows + 8, width)
    return pl.pallas_call(
        functools.partial(hole_kernel, parts),
        in_specs=[ANYWHERE] * 3,
        out_specs=WHOLE,
        out_shape=pltpu.VMEM(tiles.shape, jnp.float32),
        scratch_shapes=[
            pltpu.VMEM((pairs, pairs), jnp.float32),
            pltpu.VMEM((pairs, pairs), jnp.bfloat16),
            pltpu.VMEM((2 * pairs, pairs), jnp.bfloat16),
            pltpu.VMEM(pitched, jnp.float32),
            pltpu.VMEM(pitched, jnp.float32),
            pltpu.SemaphoreType.DMA((2,)),
            pltpu.SemaphoreType.DMA((len(parts),)),
            pltpu.SemaphoreType.DMA((len(parts),)),
        ],
        compiler_params=pltpu.CompilerParams(vmem_limit_bytes=22 * MIB),
        cost_estimate=pl.CostEstimate(
            flops=6 * pairs * pairs * rows * width, bytes_accessed=2 * tiles.size * 4, transcendentals=0
        ),
    )(in_hbm(hole_ints), in_hbm(order), in_hbm(tiles))


def ladder_kernel(first_diagonal, blocks_ref, factors_ref, core_ref, out_ref, rounded, turned, side, weighted, upper):
    _, _, rows_local, cols_local = blocks_ref.shape
    virtual, grid_points = factors_ref.shape
    col_count = virtual // cols_local
    device = lax.axis_index("row") * col_count + lax.axis_index("col")
    diagonal = (device >= first_diagonal).astype(jnp.int32)
    ratio = cols_local // rows_local
    chunk = 256
    steps = virtual // chunk

    def rows_of(i, size=chunk):
        return slice(i * size, (i + 1) * size)

    def dot(a, b):
        return jnp.dot(a, b, preferred_element_type=jnp.float32)

    def square(i, j, slot):
        tiles = [blocks_ref[(i * ratio + r) * col_count + j, slot] for r in range(ratio)]
        return jnp.concatenate(tiles, axis=0)

    def partner_of(slot):
        return jnp.where(diagonal == 1, slot, 1 - slot)

    def build(slot, step):
        partner = partner_of(slot)
        for i in range(step * chunk // cols_local, (step + 1) * chunk // cols_local):
            for j in range(col_count):
                total = square(i, j, slot) + square(j, i, partner).T
                for r in range(ratio):
                    out_ref[(i * ratio + r) * col_count + j, slot] = total[rows_of(r, rows_local), :]
                rounded[slot, rows_of(i, cols_local), rows_of(j, cols_local)] = total.astype(jnp.bfloat16)

    def turn(step):
        turned[:, rows_of(step)] = factors_ref[rows_of(step), :].T

    def left(slot, step):
        side[slot, rows_of(step), :] = dot(rounded[slot, rows_of(step), :], factors_ref[...]).astype(jnp.bfloat16)

    def block_number(i, j):
        return i * (2 * steps - i - 1) // 2 + j - i - 1

    def inner(slot, step):
        onward = slice(step * chunk, grid_points)
        product = dot(turned[rows_of(step), :], side[slot, :, onward])
        weighted[slot, rows_of(step), onward] = (core_ref[rows_of(step), onward] * product).astype(jnp.bfloat16)
        for j in range(step + 1, steps):
            upper[slot, block_number(step, j)] = product[:, rows_of(j - step)]

    def mirror(slot, step):
        for j in range(step + 1, steps):
            product = upper[partner_of(slot), block_number(step, j)].T
            weighted[slot, rows_of(j), rows_of(step)] = (core_ref[rows_of(j), rows_of(step)] * product).astype(jnp.bfloat16)

    def spread(slot, step):
        side[slot, rows_of(step), :] = dot(factors_ref[rows_of(step), :], weighted[slot]).astype(jnp.bfloat16)

    def finish(slot, step):
        product = dot(side[slot, rows_of(step), :], turned[...])
        for r in range(chunk // rows_local):
            for c in range(col_count):
                place = (step * chunk // rows_local + r) * col_count + c
                out_ref[place, slot] = out_ref[place, slot] + product[rows_of(r, rows_local), rows_of(c, cols_local)]

    build(0, 0)
    for step in range(steps):
        if step + 1 < steps:
            build(0, step + 1)
        left(0, step)
        turn(step)
    for step in range(steps):
        build(1, step)
        inner(0, step)
    for step in range(steps):
        left(1, step)
    for step in range(steps):
        inner(1, step)
        mirror(0, step)
    for step in range(steps):
        spread(0, step)
        mirror(1, step)
    for step in range(steps):
        finish(0, step)
        spread(1, step)
    for step in range(steps):
        finish(1, step)


def ladder(blocks, factors, core_matrix, first_diagonal):
    virtual, grid_points = factors.shape
    return pl.pallas_call(
        functools.partial(ladder_kernel, first_diagonal),
        in_specs=[WHOLE] * 3,
        out_specs=WHOLE,
        out_shape=pltpu.VMEM(blocks.shape, jnp.float32),
        scratch_shapes=[
            pltpu.VMEM((2, virtual, virtual), jnp.bfloat16),
            pltpu.VMEM((grid_points, virtual), jnp.bfloat16),
            pltpu.VMEM((2, virtual, grid_points), jnp.bfloat16),
            pltpu.VMEM((2, grid_points, grid_points), jnp.bfloat16),
            pltpu.VMEM((2, 6, 256, 256), jnp.float32),
        ],
        compiler_params=pltpu.CompilerParams(vmem_limit_bytes=22 * MIB),
        cost_estimate=pl.CostEstimate(
            flops=15 * virtual * virtual * grid_points, bytes_accessed=2 * blocks.size * 4, transcendentals=0
        ),
    )(in_vmem(blocks), in_vmem(factors), in_vmem(core_matrix))


def place_moves(occupied):
    moves = []
    device = 0
    for i in range(occupied - 1):
        count = occupied - 1 - i
        moves.append((device, count, 0, i, i + 1, 1))
        moves.append((device, count, 1, i + 1, i, 0))
        device += count
    for i in range(occupied):
        moves.append((device + i // 2, 1, i % 2, i, i, 1))
    return moves


def place_kernel(moves, in_ref, out_ref, sem):
    copies = []
    for n, (device, count, slot, i, j, running) in enumerate(moves):
        source = in_ref.at[pl.ds(device, count), slot]
        target = out_ref.at[i, pl.ds(j, count)] if running == 1 else out_ref.at[pl.ds(i, count), j]
        copies.append(pltpu.make_async_copy(source, target, sem.at[n]))
    for n, copy in enumerate(copies):
        copy.start(priority=n % 2)
    for copy in copies:
        copy.wait()


def place(blocks, occupied):
    moves = place_moves(occupied)
    return pl.pallas_call(
        functools.partial(place_kernel, moves),
        in_specs=[WHOLE],
        out_specs=ANYWHERE,
        out_shape=jax.ShapeDtypeStruct((occupied, occupied) + blocks.shape[2:], blocks.dtype),
        scratch_shapes=[pltpu.SemaphoreType.DMA((len(moves),))],
        compiler_params=pltpu.CompilerParams(vmem_limit_bytes=4 * MIB),
        cost_estimate=pl.CostEstimate(flops=0, bytes_accessed=2 * blocks.size * 4, transcendentals=0),
    )(in_vmem(blocks))


def exchange(blocks):
    return lax.all_to_all(blocks, AXES, split_axis=0, concat_axis=0, tiled=True)


def local(amplitudes, hole_ints, factors, core_matrix):
    row_count = lax.axis_size("row")
    col_count = lax.axis_size("col")
    devices = row_count * col_count
    occupied = amplitudes.shape[0]
    pairs = occupied * occupied
    rows_local, cols_local = amplitudes.shape[2:]
    order = np.zeros((pairs, pairs), dtype=jnp.bfloat16)
    order[np.arange(pairs), owned_pairs(occupied, devices)] = 1
    hole = hole_term(hole_ints, jnp.asarray(order), amplitudes.reshape(pairs, rows_local, cols_local))
    moved = exchange(hole.reshape(devices, 2, rows_local, cols_local))
    result = ladder(moved, factors, core_matrix, occupied * (occupied - 1) // 2)
    return place(exchange(result), occupied)


def solution(mesh):
    return jax.shard_map(
        local,
        mesh=mesh,
        in_specs=(P(None, None, "row", "col"), P(), P(), P()),
        out_specs=P(None, None, "row", "col"),
        check_vma=False,
    )
```
